512 devices in a mesh: grp: 16 (over z, core), dev: 32 (over y, x).
Axes of the slice: x: 4, y: 8, z: 8, core: 2. Of those that a mesh axis runs over, the one named last changes fastest.
Arguments:
- amplitudes: bfloat16 [1024, 256, 256], P(('grp', 'dev')), may hold values from -6 to 6
- integrals: bfloat16 [1024, 256, 256], P(('grp', 'dev')), may hold values from -6 to 6
- virt_energy: float32 [1024, 256], P(('grp', 'dev')), may hold values from 0.2 to 2
- pair_gap: float32 [1024], P(('grp', 'dev')), may hold values from 0.3 to 1.5
- rank_bucket: int32 [1024], P('grp'), may hold values from 0 to 3
- neighbours: int32 [1024, 8], P('grp'), may hold values from 0 to 63, as said below
- intersection: bfloat16 [1024, 8, 256, 256], P(('grp', 'dev')), may hold values from -0.375 to 0.375
- coupling: float32 [1024, 8], P(('grp', 'dev')), may hold values from -3 to 3
- edge_local: int32 [1024, 2], P(('grp', 'dev')), may hold values from 0 to 1
- edge_intersection: bfloat16 [1024, 2, 256, 256], P(('grp', 'dev')), may hold values from -0.375 to 0.375
- edge_coupling: float32 [1024, 2], P(('grp', 'dev')), may hold values from -3 to 3
Outputs:
- residual: float32 [1024, 256, 256], P(('grp', 'dev'))
- new_amplitudes: bfloat16 [1024, 256, 256], P(('grp', 'dev'))
The draws below stay inside these ranges and needn't reach their ends.
Inputs may be any that keep to these rules, and one draw needn't show every extreme that they name: `neighbours`: pair number n of a group is held by device n // 2 of that group. Among the 16 entries of the pairs of one device, at most 1 name pairs held by any one device; in each group some device is named exactly 1 times by the entries of every device of the group.
All inputs are finite; a program needn't handle non-finite values.
Results may differ from the reference program's by a relative error of at most 0.0049.
Values may be sent and summed in bfloat16 or wider, within the bound.
No kernel may reach another device: no remote copies, remote signals or barrier semaphores. Data moves between devices by JAX's collectives and lax.ppermute only.
A program may use at most 128 MiB of HBM per device.

```python
import math
import jax
import jax.numpy as jnp
from jax import lax

R = 256
PAIR_DEV = 2
NBR = 8
GROUPS = 16
PAIRS_GRP = 64
PAIRS = 1024
CAP = 1


def draw_neighbours(key, part):
    key = jax.random.fold_in(key, 11)
    members = PAIRS_GRP // PAIR_DEV
    groups_count = PAIRS // PAIRS_GRP
    slot_count = PAIR_DEV * NBR
    pool_size = CAP * members
    star_key, rest_key = jax.random.split(key)
    stars = jax.random.randint(star_key, (groups_count,), 0, members)
    device_keys = jax.random.split(rest_key, groups_count * members)
    device_stars = jnp.repeat(stars, members)

    def one_device(device_key, star):
        score_key, order_key, local_key = jax.random.split(device_key, 3)
        pool_ids = jnp.arange(pool_size, dtype=jnp.int32)
        scores = jax.random.permutation(score_key, pool_size).astype(jnp.int32) + jnp.where(pool_ids % members == star, -pool_size, 0).astype(jnp.int32)
        chosen = pool_ids[jnp.argsort(scores, stable=True)[:slot_count]]
        chosen = jax.random.permutation(order_key, chosen)
        local_ids = jax.random.randint(local_key, (slot_count,), 0, PAIR_DEV)
        return chosen % members * PAIR_DEV + local_ids
    neighbour_table = jax.vmap(one_device)(device_keys, device_stars)
    return neighbour_table.reshape(PAIRS, NBR).astype(jnp.int32)


def plant(entries, stream_key, smallest, top_value):
    longest = entries.shape.index(max(entries.shape))
    spots = []
    for shift in (0, 1):
        where = [jax.random.randint(jax.random.fold_in(stream_key, axis), (), 0, length) for axis, length in enumerate(entries.shape)]
        where[longest] = (where[longest] + shift) % entries.shape[longest]
        spots.append(tuple(where))
    return entries.at[spots[0]].set(smallest).at[spots[1]].set(top_value)


def steps_of(own_key, shape, cuts, smallest, high):
    gain = 1.0
    for axis_at, shards_of in cuts:
        heights = jax.random.uniform(jax.random.fold_in(jax.random.fold_in(own_key, 6), axis_at), (shards_of,), jnp.float32, smallest / len(cuts), high / len(cuts))
        gain = gain * jnp.repeat(jnp.exp(heights), shape[axis_at] // shards_of).reshape((-1,) + (1,) * (len(shape) - 1 - axis_at))
    return gain


def scatter_about(rng, shape, spread, bound, cuts=(), kind=jnp.bfloat16):
    values = jax.random.normal(rng, shape, jnp.float32) * spread
    if len(cuts) > 0:
        values = steps_of(rng, shape, cuts, -0.22, 0.18) * values
    return jnp.clip(values, min=-bound, max=bound).astype(kind)


def setup_inputs(seed: int = 0) -> dict:
    splits = jax.random.split(jax.random.key(seed), 12)
    return {
        "amplitudes": scatter_about(splits[0], (PAIRS, R, R), 1.0, 6.0, ((0, 512),)),
        "integrals": scatter_about(splits[1], (PAIRS, R, R), 1.0, 6.0, ((0, 512),)),
        "virt_energy": jnp.clip(jnp.exp(math.log(2.0) - 2.3025851 * jax.random.uniform(splits[2], (PAIRS, R), jnp.float32) ** steps_of(splits[2], (PAIRS, R), ((0, 512),), -0.2, 0.2)), 0.2, 2.0),
        "pair_gap": jnp.clip(jnp.exp(math.log(1.5) - 1.60943787 * jax.random.uniform(splits[3], (PAIRS,), jnp.float32) ** steps_of(splits[3], (PAIRS,), ((0, 512),), -0.2, 0.2)), 0.3, 1.5),
        "rank_bucket": plant(jax.random.randint(splits[4], (PAIRS,), 0, 4), jax.random.fold_in(splits[4], 1), 0, 3).astype(jnp.int32),
        "neighbours": draw_neighbours(jax.random.fold_in(splits[11], 71), 0),
        "intersection": scatter_about(splits[6], (PAIRS, NBR, R, R), R ** -0.5, 0.375, ((0, 512),)),
        "coupling": scatter_about(splits[7], (PAIRS, NBR), 0.5, 3.0, ((0, 512),), jnp.float32),
        "edge_local": plant(jax.random.randint(splits[8], (PAIRS, 2), 0, PAIR_DEV), jax.random.fold_in(splits[8], 1), 0, PAIR_DEV - 1).astype(jnp.int32),
        "edge_intersection": scatter_about(splits[9], (PAIRS, 2, R, R), R ** -0.5, 0.375, ((0, 512),)),
        "edge_coupling": scatter_about(splits[10], (PAIRS, 2), 0.5, 3.0, ((0, 512),), jnp.float32),
    }


def rounded(value):
    return lax.optimization_barrier(value.astype(jnp.bfloat16)).astype(jnp.float32)


def reference(amplitudes, integrals, virt_energy, pair_gap, rank_bucket, neighbours, intersection, coupling, edge_local, edge_intersection, edge_coupling):
    highest = lax.Precision.HIGHEST
    positions = jnp.arange(R, dtype=jnp.int32)
    rank_all = (R // 8) * jnp.left_shift(jnp.ones_like(rank_bucket), rank_bucket)
    keep_rows = positions[None, :] < rank_all[:, None]
    keep_square = keep_rows[:, :, None] & keep_rows[:, None, :]
    masked = jnp.where(keep_square, amplitudes, jnp.zeros_like(amplitudes))
    pair_ids = jnp.arange(PAIRS, dtype=jnp.int32)
    group_ids = pair_ids // PAIRS_GRP
    partner_ids = ((group_ids * PAIRS_GRP)[:, None] + neighbours).astype(jnp.int32)
    block_base = pair_ids - pair_ids % PAIR_DEV
    lower_ids = jnp.clip(block_base - PAIRS_GRP + edge_local[:, 0], 0, PAIRS - 1)
    upper_ids = jnp.clip(block_base + PAIRS_GRP + edge_local[:, 1], 0, PAIRS - 1)
    edge_ids = jnp.stack([lower_ids, upper_ids], axis=1).astype(jnp.int32)
    edge_live = jnp.stack([group_ids > 0, group_ids < GROUPS - 1], axis=1)

    def one_pair(incoming, pair):
        row_keep = keep_rows[pair][None, :, None]
        rows_full = jnp.where(row_keep, intersection[pair].astype(jnp.float32), jnp.float32(0.0))
        partner = masked[partner_ids[pair]].astype(jnp.float32)
        half_in = rounded(jnp.einsum("sab,sbc->sac", rows_full, partner, precision=highest))
        projected = jnp.einsum("sac,sdc->sad", half_in, rows_full, precision=highest)
        own_amps = masked[pair].astype(jnp.float32)
        half_out = rounded(jnp.einsum("sba,bc->sac", rows_full, own_amps, precision=highest))
        returned = rounded(coupling[pair][:, None, None] * jnp.einsum("sac,scd->sad", half_out, rows_full, precision=highest))
        incoming = incoming.at[partner_ids[pair]].add(returned)
        edge_full = jnp.where(row_keep, edge_intersection[pair].astype(jnp.float32), jnp.float32(0.0))
        edge_partner = masked[edge_ids[pair]].astype(jnp.float32)
        edge_half = rounded(jnp.einsum("sab,sbc->sac", edge_full, edge_partner, precision=highest))
        edge_proj = jnp.einsum("sac,sdc->sad", edge_half, edge_full, precision=highest)
        edge_weight = jnp.where(edge_live[pair], edge_coupling[pair], jnp.float32(0.0))
        local_term = jnp.sum(coupling[pair][:, None, None] * projected, axis=0) + jnp.sum(edge_weight[:, None, None] * edge_proj, axis=0)
        return incoming, local_term

    incoming, local_terms = lax.scan(one_pair, jnp.zeros((PAIRS, R, R), jnp.float32), pair_ids)
    denom = virt_energy[:, :, None] + virt_energy[:, None, :] + pair_gap[:, None, None]
    residual = jnp.where(keep_square, integrals.astype(jnp.float32) + denom * masked.astype(jnp.float32) - local_terms - incoming, jnp.float32(0.0))
    new_amplitudes = jnp.where(keep_square, masked.astype(jnp.float32) - residual / denom, jnp.float32(0.0)).astype(jnp.bfloat16)
    return (residual, new_amplitudes)
```

```python
import functools

import jax
import jax.numpy as jnp
from jax import lax
from jax.experimental import pallas as pl
from jax.experimental.pallas import tpu as pltpu
from jax.sharding import PartitionSpec as P

R = 256
NBR = 8
COLS = 4
ROWS = 8
BF = jnp.bfloat16
F32 = jnp.float32
LIMIT = 56 << 20

SMEM = pl.BlockSpec(memory_space=pltpu.SMEM)
VMEM = pl.BlockSpec(memory_space=pltpu.VMEM)
ANY = pl.BlockSpec(memory_space=pl.ANY)


def place():
    dev = lax.axis_index("dev")
    return dev, dev // COLS, dev % COLS


def keep_square(rank):
    rows = lax.broadcasted_iota(jnp.int32, (R, R), 0)
    cols = lax.broadcasted_iota(jnp.int32, (R, R), 1)
    return jnp.maximum(rows, cols) < rank


def return_kernel(bucket, nbr, coupling, amps, inter, masked, out, terms, sems):
    dev, _, _ = place()
    pair = pl.program_id(0)

    def copy(pair_at, entry):
        holder = nbr[2 * dev + pair_at, entry] >> 1
        slot = (holder & (COLS - 1)) * ROWS + (holder >> 2)
        index = pair_at * NBR + entry
        return pltpu.make_async_copy(terms.at[index], out.at[slot], sems.at[index])

    rank = jnp.left_shift(32, bucket[2 * dev + pair])
    own = jnp.where(keep_square(rank), amps[0].astype(F32), 0.0).astype(BF)
    masked[0] = own
    for entry in range(NBR):
        s = inter[0, entry]
        half = lax.dot_general(s, own, (((0,), (0,)), ((), ())), preferred_element_type=F32)
        term = jnp.dot(half.astype(BF), s, preferred_element_type=F32)
        terms[pair * NBR + entry] = (coupling[pair, entry] * term).astype(BF)
    for entry in range(NBR):
        copy(pair, entry).start()

    @pl.when(pair == 1)
    def _():
        for pair_at in range(2):
            for entry in range(NBR):
                copy(pair_at, entry).wait()


def select_kernel(nbr, column, out, sems):
    _, y, x = place()

    def each(act):
        for taker_x in range(COLS):

            def body(i, _):
                name = nbr[2 * (y * COLS + taker_x) + i // NBR, i % NBR]
                holder = name >> 1

                @pl.when((holder & (COLS - 1)) == x)
                def _():
                    act(
                        pltpu.make_async_copy(
                            column.at[2 * (holder >> 2) + (name & 1)],
                            out.at[taker_x * ROWS + (holder >> 2)],
                            sems.at[taker_x, i],
                        )
                    )

                return 0

            lax.fori_loop(0, 2 * NBR, body, 0)

    each(lambda copy: copy.start())
    each(lambda copy: copy.wait())


def combine_kernel(nbr, r0, r1, r2, r3, dense, table):
    _, y, x = place()

    @pl.when(pl.program_id(0) == 0)
    def _():
        for giver_x in range(COLS):
            for row in range(ROWS):
                table[giver_x, row] = 0

            def body(i, _):
                name = nbr[2 * (y * COLS + giver_x) + i // NBR, i % NBR]
                holder = name >> 1

                @pl.when((holder & (COLS - 1)) == x)
                def _():
                    table[giver_x, holder >> 2] = 1 + (name & 1)

                return 0

            lax.fori_loop(0, 2 * NBR, body, 0)

    for j in range(2):
        row = pl.program_id(0) * 2 + j
        for chunk in range(0, R, 64):
            at = pl.ds(chunk, 64)
            vals = [ref[j, at, :].astype(F32) for ref in (r0, r1, r2, r3)]
            for local in range(2):
                total = jnp.zeros((64, R), F32)
                for giver_x in range(COLS):
                    total += jnp.where(table[giver_x, row] == 1 + local, vals[giver_x], 0.0)
                dense[2 * j + local, at, :] = total.astype(BF)


def final_kernel(
    bucket,
    nbr,
    coupling,
    edge_local,
    edge_coupling,
    gap,
    masked,
    integrals,
    virt,
    inter,
    edge_inter,
    lower,
    upper,
    gathered,
    named,
    residual,
    new_amps,
    partners,
    sems,
):
    dev, _, _ = place()

    def copy(index):
        name = nbr[2 * dev + index // NBR, index % NBR]
        holder = name >> 1
        slot = (holder & (COLS - 1)) * ROWS + (holder >> 2)
        return pltpu.make_async_copy(named.at[slot], partners.at[index], sems.at[index])

    for index in range(2 * NBR):
        copy(index).start()

    def project(s, a):
        half = jnp.dot(s, a, preferred_element_type=F32).astype(BF)
        return lax.dot_general(half, s, (((1,), (1,)), ((), ())), preferred_element_type=F32)

    for pair in range(2):
        total = edge_coupling[pair, 0] * project(
            edge_inter[pair, 0], lower[edge_local[pair, 0]]
        )
        total += edge_coupling[pair, 1] * project(
            edge_inter[pair, 1], upper[edge_local[pair, 1]]
        )
        for entry in range(NBR):
            index = pair * NBR + entry
            copy(index).wait()
            total += coupling[pair, entry] * project(inter[pair, entry], partners[index])
        energy = jnp.broadcast_to(virt[pair : pair + 1, :], (R, R))
        denom = energy + energy.T + gap[pair]
        own = masked[pair].astype(F32)
        rank = jnp.left_shift(32, bucket[2 * dev + pair])
        keep = keep_square(rank)
        value = (
            integrals[pair].astype(F32) + denom * own - total - gathered[pair].astype(F32)
        )
        value = jnp.where(keep, value, 0.0)
        residual[pair] = value
        new_amps[pair] = jnp.where(keep, own - value / denom, 0.0).astype(BF)


def local(
    amplitudes,
    integrals,
    virt_energy,
    pair_gap,
    rank_bucket,
    neighbours,
    intersection,
    coupling,
    edge_local,
    edge_intersection,
    edge_coupling,
):
    groups = lax.axis_size("grp")
    devices = lax.axis_size("dev")
    columns = [[y * COLS + x for y in range(ROWS)] for x in range(COLS)]

    rows = [[y * COLS + x for x in range(COLS)] for y in range(ROWS)]

    def swap_columns(value):
        return lax.all_to_all(value, "dev", 0, 0, tiled=True, axis_index_groups=rows)

    block = jax.ShapeDtypeStruct((COLS * ROWS, R, R), BF)
    masked, outgoing = pl.pallas_call(
        return_kernel,
        grid=(2,),
        in_specs=[
            SMEM,
            SMEM,
            SMEM,
            pl.BlockSpec((1, R, R), lambda i: (i, 0, 0)),
            pl.BlockSpec((1, NBR, R, R), lambda i: (i, 0, 0, 0)),
        ],
        out_specs=[pl.BlockSpec((1, R, R), lambda i: (i, 0, 0)), ANY],
        out_shape=[jax.ShapeDtypeStruct((2, R, R), BF), block],
        scratch_shapes=[
            pltpu.VMEM((2 * NBR, R, R), BF),
            pltpu.SemaphoreType.DMA((2 * NBR,)),
        ],
        compiler_params=pltpu.CompilerParams(vmem_limit_bytes=LIMIT),
        name="returned_terms",
    )(rank_bucket, neighbours, coupling, amplitudes, intersection)
    arrived = swap_columns(outgoing)
    lower = lax.ppermute(masked, "grp", [(i, i + 1) for i in range(groups - 1)])
    upper = lax.ppermute(masked, "grp", [(i + 1, i) for i in range(groups - 1)])
    column = lax.all_gather(masked, "dev", axis=0, tiled=True, axis_index_groups=columns)
    chosen = pl.pallas_call(
        select_kernel,
        in_specs=[SMEM, VMEM],
        out_specs=ANY,
        out_shape=block,
        scratch_shapes=[pltpu.SemaphoreType.DMA((COLS, 2 * NBR))],
        compiler_params=pltpu.CompilerParams(vmem_limit_bytes=LIMIT),
        name="named_pairs",
    )(neighbours, column)
    named = swap_columns(chosen)
    dense = pl.pallas_call(
        combine_kernel,
        grid=(4,),
        in_specs=[SMEM]
        + [
            pl.BlockSpec((2, R, R), functools.partial(lambda x, i: (x * 4 + i, 0, 0), x))
            for x in range(COLS)
        ],
        out_specs=pl.BlockSpec((4, R, R), lambda i: (i, 0, 0)),
        out_shape=jax.ShapeDtypeStruct((2 * ROWS, R, R), BF),
        scratch_shapes=[pltpu.SMEM((COLS, ROWS), jnp.int32)],
        compiler_params=pltpu.CompilerParams(vmem_limit_bytes=LIMIT),
        name="column_terms",
    )(neighbours, *[arrived] * COLS)
    gathered = lax.psum_scatter(
        dense, "dev", scatter_dimension=0, tiled=True, axis_index_groups=columns
    )
    outputs = pl.pallas_call(
        final_kernel,
        in_specs=[SMEM] * 6 + [VMEM] * 8 + [ANY],
        out_specs=[VMEM, VMEM],
        out_shape=[
            jax.ShapeDtypeStruct((2, R, R), F32),
            jax.ShapeDtypeStruct((2, R, R), BF),
        ],
        scratch_shapes=[
            pltpu.VMEM((2 * NBR, R, R), BF),
            pltpu.SemaphoreType.DMA((2 * NBR,)),
        ],
        compiler_params=pltpu.CompilerParams(vmem_limit_bytes=LIMIT),
        name="residual_update",
    )(
        rank_bucket,
        neighbours,
        coupling,
        edge_local,
        edge_coupling,
        pair_gap,
        masked,
        integrals,
        virt_energy,
        intersection,
        edge_intersection,
        lower,
        upper,
        gathered,
        named,
    )
    return tuple(outputs)


def solution(mesh):
    pair = P(("grp", "dev"))
    placed = (pair, pair, pair, pair, P("grp"), P("grp")) + (pair,) * 5
    return jax.shard_map(
        local, mesh=mesh, in_specs=placed, out_specs=(pair, pair), check_vma=False
    )
```

```python
import functools

import jax
import jax.numpy as jnp
from jax import lax
from jax.experimental import pallas as pl
from jax.experimental.pallas import tpu as pltpu
from jax.sharding import PartitionSpec as P

R = 256
NBR = 8
COLS = 4
ROWS = 8
BF = jnp.bfloat16
F32 = jnp.float32
LIMIT = 56 << 20

SMEM = pl.BlockSpec(memory_space=pltpu.SMEM)
VMEM = pl.BlockSpec(memory_space=pltpu.VMEM)
ANY = pl.BlockSpec(memory_space=pl.ANY)


def place():
    dev = lax.axis_index("dev")
    return dev, dev // COLS, dev % COLS


def slot_of(holder):
    return (holder & (COLS - 1)) * ROWS + holder // COLS


def keep_square(rank):
    rows = lax.broadcasted_iota(jnp.int32, (R, R), 0)
    cols = lax.broadcasted_iota(jnp.int32, (R, R), 1)
    return jnp.maximum(rows, cols) < rank


def return_kernel(bucket, nbr, coupling, amps, inter, masked, out, terms, sems):
    dev, _, _ = place()
    pair = pl.program_id(0)

    def copy(pair_at, entry):
        slot = slot_of(nbr[entry, 2 * dev + pair_at] >> 1)
        index = pair_at * NBR + entry
        return pltpu.make_async_copy(terms.at[index], out.at[slot], sems.at[index])

    rank = jnp.left_shift(32, bucket[2 * dev + pair])
    own = jnp.where(keep_square(rank), amps[0].astype(F32), 0.0).astype(BF)
    masked[0] = own
    for entry in range(NBR):
        s = inter[0, entry]
        half = lax.dot_general(s, own, (((0,), (0,)), ((), ())), preferred_element_type=F32)
        term = jnp.dot(half.astype(BF), s, preferred_element_type=F32)
        terms[pair * NBR + entry] = (coupling[pair, entry] * term).astype(BF)
    for entry in range(NBR):
        copy(pair, entry).start()

    @pl.when(pair == 1)
    def _():
        for pair_at in range(2):
            for entry in range(NBR):
                copy(pair_at, entry).wait()


def served_kernel(nbr, served):
    _, y, x = place()
    for i in range(COLS * ROWS):
        served[i] = 0

    def note(i, _):
        giver_x, entry = i // (2 * NBR), i % (2 * NBR)
        name = nbr[entry % NBR, 2 * (y * COLS + giver_x) + entry // NBR]
        holder = name >> 1

        @pl.when((holder & (COLS - 1)) == x)
        def _():
            served[giver_x * ROWS + holder // COLS] = 1 + (name & 1)

        return 0

    lax.fori_loop(0, COLS * 2 * NBR, note, 0)


PIECES = (0, 1, -1, 2, -2, 3, -3, 4)


def select_kernel(served, *rest):
    pieces, out = rest[:ROWS], rest[ROWS]
    column, in_sems, out_sems = rest[ROWS + 1 :]
    _, y, _ = place()
    loads = []
    for at, distance in enumerate(PIECES):
        row = (y + distance) & (ROWS - 1)
        loads.append(
            pltpu.make_async_copy(
                pieces[at], column.at[pl.ds(2 * row, 2)], in_sems.at[at]
            )
        )
    for load in loads:
        load.start()
    for load in loads:
        load.wait()

    def each(act):
        def body(i, _):
            who = served[i]

            @pl.when(who > 0)
            def _():
                pair = 2 * (i & (ROWS - 1)) + who - 1
                act(pltpu.make_async_copy(column.at[pair], out.at[i], out_sems.at[i]))

            return 0

        lax.fori_loop(0, COLS * ROWS, body, 0)

    each(lambda copy: copy.start())
    each(lambda copy: copy.wait())


def combine_kernel(distances, served, arrived, *outs):
    _, y, _ = place()
    for out, group in zip(outs, distances):
        for at, distance in enumerate(group):
            row = (y + distance) & (ROWS - 1)
            totals = [jnp.zeros(out.shape[1:], F32) for _ in range(2)]
            for giver_x in range(COLS):
                value = arrived[giver_x * ROWS + row].astype(F32)
                who = served[giver_x * ROWS + row]
                for side in range(2):
                    totals[side] += jnp.where(who == 1 + side, value, 0.0)
            for side in range(2):
                out[2 * at + side] = totals[side].astype(BF)


def fold_kernel(got_up, got_down, own_up, own_down, send_up, send_down):
    send_up[...] = (own_up[...].astype(F32) + got_up[...].astype(F32)).astype(BF)
    send_down[...] = (own_down[...].astype(F32) + got_down[...].astype(F32)).astype(BF)


def final_kernel(
    bucket,
    nbr,
    coupling,
    edge_local,
    edge_coupling,
    gap,
    masked,
    integrals,
    virt,
    inter,
    edge_inter,
    lower,
    upper,
    terms0,
    terms1,
    terms2,
    terms3,
    terms4,
    terms5,
    named,
    residual,
    new_amps,
    partners,
    sems,
):
    dev, _, _ = place()
    copies = []
    for index in range(2 * NBR):
        slot = slot_of(nbr[index % NBR, 2 * dev + index // NBR] >> 1)
        copies.append(
            pltpu.make_async_copy(named.at[slot], partners.at[index], sems.at[index])
        )
    for copy in copies:
        copy.start()
    for copy in copies:
        copy.wait()

    def project(s, a):
        half = jnp.dot(s, a, preferred_element_type=F32).astype(BF)
        return lax.dot_general(half, s, (((1,), (1,)), ((), ())), preferred_element_type=F32)

    for pair in range(2):
        total = edge_coupling[pair, 0] * project(
            edge_inter[pair, 0], lower[edge_local[pair, 0]]
        )
        total += edge_coupling[pair, 1] * project(
            edge_inter[pair, 1], upper[edge_local[pair, 1]]
        )
        for entry in range(NBR):
            index = pair * NBR + entry
            total += coupling[pair, entry] * project(inter[pair, entry], partners[index])
        energy = jnp.broadcast_to(virt[pair : pair + 1, :], (R, R))
        denom = energy + energy.T + gap[pair]
        own = masked[pair].astype(F32)
        rank = jnp.left_shift(32, bucket[2 * dev + pair])
        keep = keep_square(rank)
        for ref in (terms0, terms1, terms2, terms3, terms4, terms5):
            total += ref[pair].astype(F32)
        value = integrals[pair].astype(F32) + denom * own - total
        value = jnp.where(keep, value, 0.0)
        residual[pair] = value
        new_amps[pair] = jnp.where(keep, own - value / denom, 0.0).astype(BF)


def local(
    amplitudes,
    integrals,
    virt_energy,
    pair_gap,
    rank_bucket,
    neighbours,
    intersection,
    coupling,
    edge_local,
    edge_intersection,
    edge_coupling,
):
    groups = lax.axis_size("grp")
    devices = lax.axis_size("dev")
    nbr = neighbours.T
    rows = [[y * COLS + x for x in range(COLS)] for y in range(ROWS)]

    def swap_columns(value):
        return lax.all_to_all(value, "dev", 0, 0, tiled=True, axis_index_groups=rows)

    def along_y(value, o):
        perm = [(i, (i + o * COLS) % devices) for i in range(devices)]
        return lax.ppermute(value, "dev", perm)

    block = jax.ShapeDtypeStruct((COLS * ROWS, R, R), BF)
    masked, outgoing = pl.pallas_call(
        return_kernel,
        grid=(2,),
        in_specs=[
            SMEM,
            SMEM,
            SMEM,
            pl.BlockSpec((1, R, R), lambda i: (i, 0, 0)),
            pl.BlockSpec((1, NBR, R, R), lambda i: (i, 0, 0, 0)),
        ],
        out_specs=[pl.BlockSpec((1, R, R), lambda i: (i, 0, 0)), ANY],
        out_shape=[jax.ShapeDtypeStruct((2, R, R), BF), block],
        scratch_shapes=[
            pltpu.VMEM((2 * NBR, R, R), BF),
            pltpu.SemaphoreType.DMA((2 * NBR,)),
        ],
        compiler_params=pltpu.CompilerParams(vmem_limit_bytes=LIMIT),
        name="returned_terms",
    )(rank_bucket, nbr, coupling, amplitudes, intersection)
    arrived = swap_columns(outgoing)
    lower = lax.ppermute(masked, "grp", [(i, i + 1) for i in range(groups - 1)])
    upper = lax.ppermute(masked, "grp", [(i + 1, i) for i in range(groups - 1)])
    params = pltpu.CompilerParams(vmem_limit_bytes=LIMIT)
    above2, below2 = along_y(masked, -2), along_y(masked, 2)
    above1, below1, across = along_y(masked, -1), along_y(masked, 1), along_y(masked, 4)
    served = pl.pallas_call(
        served_kernel,
        in_specs=[SMEM],
        out_specs=SMEM,
        out_shape=jax.ShapeDtypeStruct((COLS * ROWS,), jnp.int32),
        name="served_pairs",
    )(nbr)
    above3, below3 = along_y(above2, -1), along_y(below2, 1)
    pieces = (masked, above1, below1, above2, below2, above3, below3, across)
    chosen = pl.pallas_call(
        select_kernel,
        in_specs=[SMEM] + [ANY] * ROWS,
        out_specs=ANY,
        out_shape=block,
        scratch_shapes=[
            pltpu.VMEM((2 * ROWS, R, R), BF),
            pltpu.SemaphoreType.DMA((ROWS,)),
            pltpu.SemaphoreType.DMA((COLS * ROWS,)),
        ],
        compiler_params=params,
        name="named_pairs",
    )(served, *pieces)
    named = swap_columns(chosen)

    def strip(count):
        return pl.BlockSpec((count, R // 4, R), lambda i: (0, i, 0))

    def pairs(count):
        return jax.ShapeDtypeStruct((count, R, R), BF)

    def column_terms(*distances):
        return pl.pallas_call(
            functools.partial(combine_kernel, distances),
            grid=(4,),
            in_specs=[SMEM, strip(COLS * ROWS)],
            out_specs=[strip(2 * len(group)) for group in distances],
            out_shape=[pairs(2 * len(group)) for group in distances],
            compiler_params=params,
            name="column_terms",
        )(served, arrived)

    up, down, across_terms = column_terms((1, 3), (-1, -3), (4,))
    got_up, got_down = along_y(up, 1), along_y(down, -1)
    got_across = along_y(across_terms, 4)
    own, own_up, own_down = column_terms((0,), (2,), (-2,))
    first = pl.BlockSpec((2, R, R), lambda i: (0, 0, 0))
    second = pl.BlockSpec((2, R, R), lambda i: (1, 0, 0))
    send_up, send_down = pl.pallas_call(
        fold_kernel,
        grid=(1,),
        in_specs=[second, second, first, first],
        out_specs=[first, first],
        out_shape=[pairs(2)] * 2,
        compiler_params=params,
        name="folded_terms",
    )(got_up, got_down, own_up, own_down)
    terms = [own, got_up, got_down, got_across, along_y(send_up, 2), along_y(send_down, -2)]
    outputs = pl.pallas_call(
        final_kernel,
        grid=(1,),
        in_specs=[SMEM] * 6 + [VMEM] * 7 + [first] * 6 + [ANY],
        out_specs=[VMEM, VMEM],
        out_shape=[
            jax.ShapeDtypeStruct((2, R, R), F32),
            jax.ShapeDtypeStruct((2, R, R), BF),
        ],
        scratch_shapes=[
            pltpu.VMEM((2 * NBR, R, R), BF),
            pltpu.SemaphoreType.DMA((2 * NBR,)),
        ],
        compiler_params=pltpu.CompilerParams(vmem_limit_bytes=LIMIT),
        name="residual_update",
    )(
        rank_bucket,
        nbr,
        coupling,
        edge_local,
        edge_coupling,
        pair_gap,
        masked,
        integrals,
        virt_energy,
        intersection,
        edge_intersection,
        lower,
        upper,
        *terms,
        named,
    )
    return tuple(outputs)


def solution(mesh):
    pair = P(("grp", "dev"))
    placed = (pair, pair, pair, pair, P("grp"), P("grp")) + (pair,) * 5
    return jax.shard_map(
        local, mesh=mesh, in_specs=placed, out_specs=(pair, pair), check_vma=False
    )
```

```python
import functools

import jax
import jax.numpy as jnp
from jax import lax
from jax.experimental import pallas as pl
from jax.experimental.pallas import tpu as pltpu
from jax.sharding import PartitionSpec as P

R = 256
NBR = 8
COLS = 4
ROWS = 8
BF = jnp.bfloat16
F32 = jnp.float32
LIMIT = 56 << 20

SMEM = pl.BlockSpec(memory_space=pltpu.SMEM)
VMEM = pl.BlockSpec(memory_space=pltpu.VMEM)
ANY = pl.BlockSpec(memory_space=pl.ANY)


def place():
    dev = lax.axis_index("dev")
    return dev, dev // COLS, dev % COLS


def slot_of(holder):
    return (holder & (COLS - 1)) * ROWS + holder // COLS


def keep_square(rank):
    rows = lax.broadcasted_iota(jnp.int32, (R, R), 0)
    cols = lax.broadcasted_iota(jnp.int32, (R, R), 1)
    return jnp.maximum(rows, cols) < rank


def times_transposed(a, b):
    return lax.dot_general(a, b, (((1,), (1,)), ((), ())), preferred_element_type=F32)


def return_kernel(bucket, nbr, coupling, amps, inter, masked, out, terms, sems):
    dev, _, _ = place()
    pair = pl.program_id(0)

    def copy(pair_at, entry):
        slot = slot_of(nbr[entry, 2 * dev + pair_at] >> 1)
        index = pair_at * NBR + entry
        return pltpu.make_async_copy(terms.at[index], out.at[slot], sems.at[index])

    rank = jnp.left_shift(32, bucket[2 * dev + pair])
    own = jnp.where(keep_square(rank), amps[0].astype(F32), 0.0).astype(BF)
    masked[0] = own
    for entry in range(NBR):
        s = inter[0, entry]
        half = lax.dot_general(s, own, (((0,), (0,)), ((), ())), preferred_element_type=F32)
        term = jnp.dot(half.astype(BF), s, preferred_element_type=F32)
        terms[pair * NBR + entry] = (coupling[pair, entry] * term).astype(BF)
    for entry in range(NBR):
        copy(pair, entry).start()

    @pl.when(pair == 1)
    def _():
        for pair_at in range(2):
            for entry in range(NBR):
                copy(pair_at, entry).wait()


def served_kernel(nbr, served):
    _, y, x = place()
    spare = COLS * ROWS
    for i in range(spare):
        served[i] = 0
    for giver_x in range(COLS):
        for entry in range(2 * NBR):
            name = nbr[entry % NBR, 2 * (y * COLS + giver_x) + entry // NBR]
            holder = name >> 1
            hit = (holder & (COLS - 1)) == x
            at = jnp.where(hit, giver_x * ROWS + (holder >> 2), spare)
            served[at] = 1 + (name & 1)


PIECES = (0, 1, -1, 2, -2, 3, -3)


def select_kernel(served, *rest):
    pieces, out = rest[: ROWS + 1], rest[ROWS + 1]
    column, in_sems, out_sems = rest[ROWS + 2 :]
    _, y, _ = place()
    loads = []
    for at, distance in enumerate(PIECES):
        row = (y + distance) & (ROWS - 1)
        loads.append(
            pltpu.make_async_copy(
                pieces[at], column.at[pl.ds(2 * row, 2)], in_sems.at[at]
            )
        )
    far = (y + ROWS // 2) & (ROWS - 1)
    for side in range(2):
        at = ROWS - 1 + side
        rows = column.at[pl.ds(2 * far + side, 1)]
        loads.append(pltpu.make_async_copy(pieces[at], rows, in_sems.at[at]))
    for load in loads:
        load.start()
    for load in loads:
        load.wait()

    def each(act):
        def body(i, _):
            who = served[i]

            @pl.when(who > 0)
            def _():
                pair = 2 * (i & (ROWS - 1)) + who - 1
                act(pltpu.make_async_copy(column.at[pair], out.at[i], out_sems.at[i]))

            return 0

        lax.fori_loop(0, COLS * ROWS, body, 0)

    each(lambda copy: copy.start())
    each(lambda copy: copy.wait())


def combine_kernel(distances, served, arrived, *rest):
    outs, (slots, sems) = rest[: len(distances)], rest[len(distances) :]
    _, y, _ = place()
    order = [distance for group in distances for distance, _ in group]

    def fetches(at, act):
        row = (y + order[at]) & (ROWS - 1)
        for giver_x in range(COLS):
            copy = pltpu.make_async_copy(
                arrived.at[giver_x * ROWS + row],
                slots.at[at * COLS + giver_x],
                sems.at[at * COLS + giver_x],
            )
            pl.when(served[giver_x * ROWS + row] > 0)(functools.partial(act, copy))

    for at in range(len(order)):
        fetches(at, lambda copy: copy.start())
    at = 0
    for out, group in zip(outs, distances):
        put = 0
        for distance, sides in group:
            fetches(at, lambda copy: copy.wait())
            row = (y + distance) & (ROWS - 1)
            for chunk in range(0, R, 64):
                part = pl.ds(chunk, 64)
                totals = [jnp.zeros((64, R), F32) for _ in sides]
                for giver_x in range(COLS):
                    value = slots[at * COLS + giver_x, part, :].astype(F32)
                    who = served[giver_x * ROWS + row]
                    for i, side in enumerate(sides):
                        totals[i] += jnp.where(who == 1 + side, value, 0.0)
                for i, total in enumerate(totals):
                    out[put + i, part, :] = total.astype(BF)
            put += len(sides)
            at += 1


def fold_kernel(got_up, got_down, far_up, far_down, own_up, own_down, send_up, send_down):
    for side in range(2):
        ups = own_up[side].astype(F32) + got_up[side].astype(F32)
        downs = own_down[side].astype(F32) + got_down[side].astype(F32)
        if side == 0:
            ups += far_up[0].astype(F32)
        else:
            downs += far_down[0].astype(F32)
        send_up[side] = ups.astype(BF)
        send_down[side] = downs.astype(BF)


def project(s, a):
    half = jnp.dot(s, a, preferred_element_type=F32).astype(BF)
    return times_transposed(half, s)


def gap_matrix(virt, gap, pair):
    energy = jnp.broadcast_to(virt[pl.ds(pair, 1), :], (R, R))
    return energy + energy.T + gap[pair]


def edge_kernel(
    edge_local, edge_coupling, gap, masked, integrals, virt, edge_inter, lower, upper, partial
):
    pair = pl.program_id(0)
    total = edge_coupling[pair, 0] * project(edge_inter[0, 0], lower[edge_local[pair, 0]])
    total += edge_coupling[pair, 1] * project(edge_inter[0, 1], upper[edge_local[pair, 1]])
    own = masked[0].astype(F32)
    partial[0] = integrals[0].astype(F32) + gap_matrix(virt, gap, pair) * own - total


def final_kernel(bucket, nbr, coupling, gap, masked, partial, virt, inter, *rest):
    terms, (named, residual, new_amps, partners, sems) = rest[:-5], rest[-5:]
    dev, _, _ = place()
    pair = pl.program_id(0)

    def partner_copy(index, entry):
        slot = slot_of(nbr[entry, 2 * dev + index // NBR] >> 1)
        return pltpu.make_async_copy(named.at[slot], partners.at[index], sems.at[index])

    @pl.when(pair == 0)
    def _():
        for index in range(2 * NBR):
            partner_copy(index, index % NBR).start()

    for entry in range(NBR):
        partner_copy(pair * NBR + entry, entry).wait()

    total = terms[0][0].astype(F32)
    for ref in terms[1:]:
        total += ref[0].astype(F32)
    for entry in range(NBR):
        total += coupling[pair, entry] * project(inter[0, entry], partners[pair * NBR + entry])
    keep = keep_square(jnp.left_shift(32, bucket[2 * dev + pair]))
    value = jnp.where(keep, partial[0] - total, 0.0)
    residual[0] = value
    change = value / gap_matrix(virt, gap, pair)
    new_amps[0] = jnp.where(keep, masked[0].astype(F32) - change, 0.0).astype(BF)


def local(
    amplitudes,
    integrals,
    virt_energy,
    pair_gap,
    rank_bucket,
    neighbours,
    intersection,
    coupling,
    edge_local,
    edge_intersection,
    edge_coupling,
):
    groups = lax.axis_size("grp")
    devices = lax.axis_size("dev")
    nbr = neighbours.T
    rows = [[y * COLS + x for x in range(COLS)] for y in range(ROWS)]

    def swap_columns(value):
        return lax.all_to_all(value, "dev", 0, 0, tiled=True, axis_index_groups=rows)

    def along_y(value, o):
        perm = [(i, (i + o * COLS) % devices) for i in range(devices)]
        return lax.ppermute(value, "dev", perm)

    block = jax.ShapeDtypeStruct((COLS * ROWS, R, R), BF)
    masked, outgoing = pl.pallas_call(
        return_kernel,
        grid=(2,),
        in_specs=[
            SMEM,
            SMEM,
            SMEM,
            pl.BlockSpec((1, R, R), lambda i: (i, 0, 0)),
            pl.BlockSpec((1, NBR, R, R), lambda i: (i, 0, 0, 0)),
        ],
        out_specs=[pl.BlockSpec((1, R, R), lambda i: (i, 0, 0)), ANY],
        out_shape=[jax.ShapeDtypeStruct((2, R, R), BF), block],
        scratch_shapes=[
            pltpu.VMEM((2 * NBR, R, R), BF),
            pltpu.SemaphoreType.DMA((2 * NBR,)),
        ],
        compiler_params=pltpu.CompilerParams(vmem_limit_bytes=LIMIT),
        name="returned_terms",
    )(rank_bucket, nbr, coupling, amplitudes, intersection)
    arrived = swap_columns(outgoing)
    params = pltpu.CompilerParams(vmem_limit_bytes=LIMIT)
    above2, below2 = along_y(masked, -2), along_y(masked, 2)
    above1, below1 = along_y(masked, -1), along_y(masked, 1)
    served = pl.pallas_call(
        served_kernel,
        in_specs=[SMEM],
        out_specs=SMEM,
        out_shape=jax.ShapeDtypeStruct((COLS * ROWS + 1,), jnp.int32),
        name="served_pairs",
    )(nbr)
    above3, below3 = along_y(above2, -1), along_y(below2, 1)
    above4, below4 = along_y(above2[:1], -2), along_y(below2[1:], 2)
    pieces = (masked, above1, below1, above2, below2, above3, below3, above4, below4)
    chosen = pl.pallas_call(
        select_kernel,
        in_specs=[SMEM] + [ANY] * (ROWS + 1),
        out_specs=ANY,
        out_shape=block,
        scratch_shapes=[
            pltpu.VMEM((2 * ROWS, R, R), BF),
            pltpu.SemaphoreType.DMA((ROWS + 1,)),
            pltpu.SemaphoreType.DMA((COLS * ROWS,)),
        ],
        compiler_params=params,
        name="named_pairs",
    )(served, *pieces)
    lower = lax.ppermute(masked, "grp", [(i, i + 1) for i in range(groups - 1)])
    upper = lax.ppermute(masked, "grp", [(i + 1, i) for i in range(groups - 1)])
    named = swap_columns(chosen)

    def pairs(count):
        return jax.ShapeDtypeStruct((count, R, R), BF)

    def column_terms(*groups):
        counts = [sum(len(sides) for _, sides in group) for group in groups]
        rows_in = COLS * sum(len(group) for group in groups)
        return pl.pallas_call(
            functools.partial(combine_kernel, groups),
            in_specs=[SMEM, ANY],
            out_specs=[VMEM] * len(groups),
            out_shape=[pairs(count) for count in counts],
            scratch_shapes=[
                pltpu.VMEM((rows_in, R, R), BF),
                pltpu.SemaphoreType.DMA((rows_in,)),
            ],
            compiler_params=params,
            name="column_terms",
        )(served, arrived)

    both = (0, 1)
    up, down, far_up, far_down = column_terms(
        ((1, both), (3, both)), ((-1, both), (-3, both)), ((4, (0,)),), ((4, (1,)),)
    )
    got_up, got_down = along_y(up, 1), along_y(down, -1)
    got_far_up, got_far_down = along_y(far_up, 2), along_y(far_down, -2)
    own, own_up, own_down = column_terms(((0, both),), ((2, both),), ((-2, both),))
    single = pl.BlockSpec((1, R, R), lambda i: (0, 0, 0))
    first = pl.BlockSpec((2, R, R), lambda i: (0, 0, 0))
    second = pl.BlockSpec((2, R, R), lambda i: (1, 0, 0))
    send_up, send_down = pl.pallas_call(
        fold_kernel,
        grid=(1,),
        in_specs=[second, second, single, single, first, first],
        out_specs=[first, first],
        out_shape=[pairs(2)] * 2,
        compiler_params=params,
        name="folded_terms",
    )(got_up, got_down, got_far_up, got_far_down, own_up, own_down)
    terms = [own, got_up, got_down, along_y(send_up, 2), along_y(send_down, -2)]
    each = pl.BlockSpec((1, R, R), lambda i: (i, 0, 0))

    def each_of(count):
        return pl.BlockSpec((1, count, R, R), lambda i: (i, 0, 0, 0))

    partial = pl.pallas_call(
        edge_kernel,
        grid=(2,),
        in_specs=[SMEM] * 3 + [each, each, VMEM, each_of(2), VMEM, VMEM],
        out_specs=each,
        out_shape=jax.ShapeDtypeStruct((2, R, R), F32),
        compiler_params=params,
        name="edges",
    )(
        edge_local,
        edge_coupling,
        pair_gap,
        masked,
        integrals,
        virt_energy,
        edge_intersection,
        lower,
        upper,
    )
    outputs = pl.pallas_call(
        final_kernel,
        grid=(2,),
        in_specs=[SMEM] * 4 + [each, each, VMEM, each_of(NBR)] + [each] * len(terms) + [ANY],
        out_specs=[each, each],
        out_shape=[
            jax.ShapeDtypeStruct((2, R, R), F32),
            jax.ShapeDtypeStruct((2, R, R), BF),
        ],
        scratch_shapes=[
            pltpu.VMEM((2 * NBR, R, R), BF),
            pltpu.SemaphoreType.DMA((2 * NBR,)),
        ],
        compiler_params=params,
        name="residual_update",
    )(
        rank_bucket,
        nbr,
        coupling,
        pair_gap,
        masked,
        partial,
        virt_energy,
        intersection,
        *terms,
        named,
    )
    return tuple(outputs)


def solution(mesh):
    pair = P(("grp", "dev"))
    placed = (pair, pair, pair, pair, P("grp"), P("grp")) + (pair,) * 5
    return jax.shard_map(
        local, mesh=mesh, in_specs=placed, out_specs=(pair, pair), check_vma=False
    )
```

```python
import functools

import jax
import jax.numpy as jnp
from jax import lax
from jax.experimental import pallas as pl
from jax.experimental.pallas import tpu as pltpu
from jax.sharding import PartitionSpec as P

R = 256
NBR = 8
COLS = 4
ROWS = 8
BF = jnp.bfloat16
F32 = jnp.float32
LIMIT = 56 << 20

SMEM = pl.BlockSpec(memory_space=pltpu.SMEM)
VMEM = pl.BlockSpec(memory_space=pltpu.VMEM)
ANY = pl.BlockSpec(memory_space=pl.ANY)


def place():
    dev = lax.axis_index("dev")
    return dev, dev // COLS, dev % COLS


def slot_of(holder):
    return (holder & (COLS - 1)) * ROWS + holder // COLS


def keep_square(rank):
    rows = lax.broadcasted_iota(jnp.int32, (R, R), 0)
    cols = lax.broadcasted_iota(jnp.int32, (R, R), 1)
    return jnp.maximum(rows, cols) < rank


def times_transposed(a, b):
    return lax.dot_general(a, b, (((1,), (1,)), ((), ())), preferred_element_type=F32)


def return_kernel(bucket, nbr, coupling, amps, inter, masked, out, terms, sems):
    dev, _, _ = place()
    pair = pl.program_id(0)

    def copy(pair_at, entry):
        slot = slot_of(nbr[entry, 2 * dev + pair_at] >> 1)
        index = pair_at * NBR + entry
        return pltpu.make_async_copy(terms.at[index], out.at[slot], sems.at[index])

    rank = jnp.left_shift(32, bucket[2 * dev + pair])
    own = jnp.where(keep_square(rank), amps[0].astype(F32), 0.0).astype(BF)
    masked[0] = own
    halves = []
    for entry in range(NBR):
        half = lax.dot_general(
            inter[0, entry], own, (((0,), (0,)), ((), ())), preferred_element_type=F32
        )
        halves.append(half.astype(BF))
    for entry in range(NBR):
        term = jnp.dot(halves[entry], inter[0, entry], preferred_element_type=F32)
        terms[pair * NBR + entry] = (coupling[pair, entry] * term).astype(BF)
    for entry in range(NBR):
        copy(pair, entry).start()

    @pl.when(pair == 1)
    def _():
        for pair_at in range(2):
            for entry in range(NBR):
                copy(pair_at, entry).wait()


def served_kernel(nbr, served):
    _, y, x = place()
    spare = COLS * ROWS
    for i in range(spare):
        served[i] = 0
    for giver_x in range(COLS):
        for entry in range(2 * NBR):
            name = nbr[entry % NBR, 2 * (y * COLS + giver_x) + entry // NBR]
            holder = name >> 1
            hit = (holder & (COLS - 1)) == x
            at = jnp.where(hit, giver_x * ROWS + (holder >> 2), spare)
            served[at] = 1 + (name & 1)


PIECES = (0, 1, -1, 2, -2, 3, -3)


def select_kernel(served, *rest):
    pieces, out = rest[: ROWS + 1], rest[ROWS + 1]
    column, in_sems, out_sems = rest[ROWS + 2 :]
    _, y, _ = place()
    loads = []
    for at, distance in enumerate(PIECES):
        row = (y + distance) & (ROWS - 1)
        loads.append(
            pltpu.make_async_copy(
                pieces[at], column.at[pl.ds(2 * row, 2)], in_sems.at[at]
            )
        )
    far = (y + ROWS // 2) & (ROWS - 1)
    for side in range(2):
        at = ROWS - 1 + side
        rows = column.at[pl.ds(2 * far + side, 1)]
        loads.append(pltpu.make_async_copy(pieces[at], rows, in_sems.at[at]))
    for load in loads:
        load.start()
    for load in loads:
        load.wait()

    def each(act):
        def body(i, _):
            who = served[i]

            @pl.when(who > 0)
            def _():
                pair = 2 * (i & (ROWS - 1)) + who - 1
                act(pltpu.make_async_copy(column.at[pair], out.at[i], out_sems.at[i]))

            return 0

        lax.fori_loop(0, COLS * ROWS, body, 0)

    each(lambda copy: copy.start())
    each(lambda copy: copy.wait())


def combine_kernel(distances, served, arrived, *rest):
    outs, (slots, sems) = rest[: len(distances)], rest[len(distances) :]
    _, y, _ = place()
    order = [distance for group in distances for distance, _ in group]

    def fetches(at, act):
        row = (y + order[at]) & (ROWS - 1)
        for giver_x in range(COLS):
            copy = pltpu.make_async_copy(
                arrived.at[giver_x * ROWS + row],
                slots.at[at * COLS + giver_x],
                sems.at[at * COLS + giver_x],
            )
            pl.when(served[giver_x * ROWS + row] > 0)(functools.partial(act, copy))

    for at in range(len(order)):
        fetches(at, lambda copy: copy.start())
    at = 0
    for out, group in zip(outs, distances):
        put = 0
        for distance, sides in group:
            fetches(at, lambda copy: copy.wait())
            row = (y + distance) & (ROWS - 1)
            for chunk in range(0, R, 64):
                part = pl.ds(chunk, 64)
                totals = [jnp.zeros((64, R), F32) for _ in sides]
                for giver_x in range(COLS):
                    value = slots[at * COLS + giver_x, part, :].astype(F32)
                    who = served[giver_x * ROWS + row]
                    for i, side in enumerate(sides):
                        totals[i] += jnp.where(who == 1 + side, value, 0.0)
                for i, total in enumerate(totals):
                    out[put + i, part, :] = total.astype(BF)
            put += len(sides)
            at += 1


def fold_kernel(got_up, got_down, far_up, far_down, own_up, own_down, send_up, send_down):
    for side in range(2):
        ups = own_up[side].astype(F32) + got_up[side].astype(F32)
        downs = own_down[side].astype(F32) + got_down[side].astype(F32)
        if side == 0:
            ups += far_up[0].astype(F32)
        else:
            downs += far_down[0].astype(F32)
        send_up[side] = ups.astype(BF)
        send_down[side] = downs.astype(BF)


def project(s, a):
    half = jnp.dot(s, a, preferred_element_type=F32).astype(BF)
    return times_transposed(half, s)


def gap_matrix(virt, gap, pair):
    energy = jnp.broadcast_to(virt[pl.ds(pair, 1), :], (R, R))
    return energy + energy.T + gap[pair]


def edge_kernel(
    edge_local, edge_coupling, gap, masked, integrals, virt, edge_inter, lower, upper, partial
):
    pair = pl.program_id(0)
    total = edge_coupling[pair, 0] * project(edge_inter[0, 0], lower[edge_local[pair, 0]])
    total += edge_coupling[pair, 1] * project(edge_inter[0, 1], upper[edge_local[pair, 1]])
    own = masked[0].astype(F32)
    partial[0] = integrals[0].astype(F32) + gap_matrix(virt, gap, pair) * own - total


def final_kernel(bucket, nbr, coupling, gap, masked, partial, virt, inter, *rest):
    terms, (named, residual, new_amps, partners, sems) = rest[:-5], rest[-5:]
    dev, _, _ = place()
    pair = pl.program_id(0)

    def partner_copy(index, entry):
        slot = slot_of(nbr[entry, 2 * dev + index // NBR] >> 1)
        return pltpu.make_async_copy(named.at[slot], partners.at[index], sems.at[index])

    @pl.when(pair == 0)
    def _():
        for index in range(2 * NBR):
            partner_copy(index, index % NBR).start()

    for entry in range(NBR):
        partner_copy(pair * NBR + entry, entry).wait()

    total = terms[0][0].astype(F32)
    for ref in terms[1:]:
        total += ref[0].astype(F32)
    for entry in range(NBR):
        total += coupling[pair, entry] * project(inter[0, entry], partners[pair * NBR + entry])
    keep = keep_square(jnp.left_shift(32, bucket[2 * dev + pair]))
    value = jnp.where(keep, partial[0] - total, 0.0)
    residual[0] = value
    change = value / gap_matrix(virt, gap, pair)
    new_amps[0] = jnp.where(keep, masked[0].astype(F32) - change, 0.0).astype(BF)


def local(
    amplitudes,
    integrals,
    virt_energy,
    pair_gap,
    rank_bucket,
    neighbours,
    intersection,
    coupling,
    edge_local,
    edge_intersection,
    edge_coupling,
):
    groups = lax.axis_size("grp")
    devices = lax.axis_size("dev")
    nbr = neighbours.T
    rows = [[y * COLS + x for x in range(COLS)] for y in range(ROWS)]

    def swap_columns(value):
        return lax.all_to_all(value, "dev", 0, 0, tiled=True, axis_index_groups=rows)

    def along_y(value, o):
        perm = [(i, (i + o * COLS) % devices) for i in range(devices)]
        return lax.ppermute(value, "dev", perm)

    block = jax.ShapeDtypeStruct((COLS * ROWS, R, R), BF)
    masked, outgoing = pl.pallas_call(
        return_kernel,
        grid=(2,),
        in_specs=[
            SMEM,
            SMEM,
            SMEM,
            pl.BlockSpec((1, R, R), lambda i: (i, 0, 0)),
            pl.BlockSpec((1, NBR, R, R), lambda i: (i, 0, 0, 0)),
        ],
        out_specs=[pl.BlockSpec((1, R, R), lambda i: (i, 0, 0)), ANY],
        out_shape=[jax.ShapeDtypeStruct((2, R, R), BF), block],
        scratch_shapes=[
            pltpu.VMEM((2 * NBR, R, R), BF),
            pltpu.SemaphoreType.DMA((2 * NBR,)),
        ],
        compiler_params=pltpu.CompilerParams(vmem_limit_bytes=LIMIT),
        name="returned_terms",
    )(rank_bucket, nbr, coupling, amplitudes, intersection)
    arrived = swap_columns(outgoing)
    params = pltpu.CompilerParams(vmem_limit_bytes=LIMIT)
    above2, below2 = along_y(masked, -2), along_y(masked, 2)
    above1, below1 = along_y(masked, -1), along_y(masked, 1)
    served = pl.pallas_call(
        served_kernel,
        in_specs=[SMEM],
        out_specs=SMEM,
        out_shape=jax.ShapeDtypeStruct((COLS * ROWS + 1,), jnp.int32),
        name="served_pairs",
    )(nbr)
    above3, below3 = along_y(above2, -1), along_y(below2, 1)
    above4, below4 = along_y(above2[:1], -2), along_y(below2[1:], 2)
    pieces = (masked, above1, below1, above2, below2, above3, below3, above4, below4)
    lower = lax.ppermute(masked, "grp", [(i, i + 1) for i in range(groups - 1)])
    upper = lax.ppermute(masked, "grp", [(i + 1, i) for i in range(groups - 1)])
    served, lower, upper = lax.optimization_barrier((served, lower, upper))
    chosen = pl.pallas_call(
        select_kernel,
        in_specs=[SMEM] + [ANY] * (ROWS + 1),
        out_specs=ANY,
        out_shape=block,
        scratch_shapes=[
            pltpu.VMEM((2 * ROWS, R, R), BF),
            pltpu.SemaphoreType.DMA((ROWS + 1,)),
            pltpu.SemaphoreType.DMA((COLS * ROWS,)),
        ],
        compiler_params=params,
        name="named_pairs",
    )(served, *pieces)
    named = swap_columns(chosen)

    def pairs(count):
        return jax.ShapeDtypeStruct((count, R, R), BF)

    def column_terms(*groups):
        counts = [sum(len(sides) for _, sides in group) for group in groups]
        rows_in = COLS * sum(len(group) for group in groups)
        return pl.pallas_call(
            functools.partial(combine_kernel, groups),
            in_specs=[SMEM, ANY],
            out_specs=[VMEM] * len(groups),
            out_shape=[pairs(count) for count in counts],
            scratch_shapes=[
                pltpu.VMEM((rows_in, R, R), BF),
                pltpu.SemaphoreType.DMA((rows_in,)),
            ],
            compiler_params=pltpu.CompilerParams(vmem_limit_bytes=16 << 20),
            name="column_terms",
        )(served, arrived)

    both = (0, 1)
    up, down, far_up, far_down = column_terms(
        ((1, both), (3, both)), ((-1, both), (-3, both)), ((4, (0,)),), ((4, (1,)),)
    )
    got_up, got_down = along_y(up, 1), along_y(down, -1)
    got_far_up, got_far_down = along_y(far_up, 2), along_y(far_down, -2)
    own, own_up, own_down = column_terms(((0, both),), ((2, both),), ((-2, both),))
    single = pl.BlockSpec((1, R, R), lambda i: (0, 0, 0))
    first = pl.BlockSpec((2, R, R), lambda i: (0, 0, 0))
    second = pl.BlockSpec((2, R, R), lambda i: (1, 0, 0))
    send_up, send_down = pl.pallas_call(
        fold_kernel,
        grid=(1,),
        in_specs=[second, second, single, single, first, first],
        out_specs=[first, first],
        out_shape=[pairs(2)] * 2,
        compiler_params=pltpu.CompilerParams(vmem_limit_bytes=12 << 20),
        name="folded_terms",
    )(got_up, got_down, got_far_up, got_far_down, own_up, own_down)
    terms = [own, got_up, got_down, along_y(send_up, 2), along_y(send_down, -2)]
    each = pl.BlockSpec((1, R, R), lambda i: (i, 0, 0))

    def each_of(count):
        return pl.BlockSpec((1, count, R, R), lambda i: (i, 0, 0, 0))

    partial = pl.pallas_call(
        edge_kernel,
        grid=(2,),
        in_specs=[SMEM] * 3 + [each, each, VMEM, each_of(2), VMEM, VMEM],
        out_specs=each,
        out_shape=jax.ShapeDtypeStruct((2, R, R), F32),
        compiler_params=params,
        name="edges",
    )(
        edge_local,
        edge_coupling,
        pair_gap,
        masked,
        integrals,
        virt_energy,
        edge_intersection,
        lower,
        upper,
    )
    outputs = pl.pallas_call(
        final_kernel,
        grid=(2,),
        in_specs=[SMEM] * 4 + [each, each, VMEM, each_of(NBR)] + [each] * len(terms) + [ANY],
        out_specs=[each, each],
        out_shape=[
            jax.ShapeDtypeStruct((2, R, R), F32),
            jax.ShapeDtypeStruct((2, R, R), BF),
        ],
        scratch_shapes=[
            pltpu.VMEM((2 * NBR, R, R), BF),
            pltpu.SemaphoreType.DMA((2 * NBR,)),
        ],
        compiler_params=params,
        name="residual_update",
    )(
        rank_bucket,
        nbr,
        coupling,
        pair_gap,
        masked,
        partial,
        virt_energy,
        intersection,
        *terms,
        named,
    )
    return tuple(outputs)


def solution(mesh):
    pair = P(("grp", "dev"))
    placed = (pair, pair, pair, pair, P("grp"), P("grp")) + (pair,) * 5
    return jax.shard_map(
        local, mesh=mesh, in_specs=placed, out_specs=(pair, pair), check_vma=False
    )
```

```python
import functools

import jax
import jax.numpy as jnp
from jax import lax
from jax.experimental import pallas as pl
from jax.experimental.pallas import tpu as pltpu
from jax.sharding import PartitionSpec as P

R = 256
NBR = 8
COLS = 4
ROWS = 8
BF = jnp.bfloat16
F32 = jnp.float32
LIMIT = 56 << 20

SMEM = pl.BlockSpec(memory_space=pltpu.SMEM)
VMEM = pl.BlockSpec(memory_space=pltpu.VMEM)
ANY = pl.BlockSpec(memory_space=pl.ANY)


def place():
    dev = lax.axis_index("dev")
    return dev, dev // COLS, dev % COLS


def slot_of(holder):
    return (holder & (COLS - 1)) * ROWS + holder // COLS


def keep_square(rank):
    rows = lax.broadcasted_iota(jnp.int32, (R, R), 0)
    cols = lax.broadcasted_iota(jnp.int32, (R, R), 1)
    return jnp.maximum(rows, cols) < rank


def times_transposed(a, b):
    return lax.dot_general(a, b, (((1,), (1,)), ((), ())), preferred_element_type=F32)


def return_kernel(bucket, nbr, coupling, amps, inter, masked, out, terms, sems):
    dev, _, _ = place()
    pair = pl.program_id(0)

    def copy(pair_at, entry):
        slot = slot_of(nbr[entry, 2 * dev + pair_at] >> 1)
        index = pair_at * NBR + entry
        return pltpu.make_async_copy(terms.at[index], out.at[slot], sems.at[index])

    rank = jnp.left_shift(32, bucket[2 * dev + pair])
    own = jnp.where(keep_square(rank), amps[0].astype(F32), 0.0).astype(BF)
    masked[0] = own
    halves = []
    for entry in range(NBR):
        half = lax.dot_general(
            inter[0, entry], own, (((0,), (0,)), ((), ())), preferred_element_type=F32
        )
        halves.append(half.astype(BF))
    for entry in range(NBR):
        term = jnp.dot(halves[entry], inter[0, entry], preferred_element_type=F32)
        terms[pair * NBR + entry] = (coupling[pair, entry] * term).astype(BF)
        copy(pair, entry).start()

    @pl.when(pair == 1)
    def _():
        for pair_at in range(2):
            for entry in range(NBR):
                copy(pair_at, entry).wait()


def served_kernel(nbr, served):
    _, y, x = place()
    spare = COLS * ROWS
    for i in range(spare):
        served[i] = 0
    for giver_x in range(COLS):
        for entry in range(2 * NBR):
            name = nbr[entry % NBR, 2 * (y * COLS + giver_x) + entry // NBR]
            holder = name >> 1
            hit = (holder & (COLS - 1)) == x
            at = jnp.where(hit, giver_x * ROWS + (holder >> 2), spare)
            served[at] = 1 + (name & 1)


PIECES = (0, 1, -1, 2, -2, 3, -3)


def select_kernel(served, *rest):
    pieces, out = rest[: ROWS + 1], rest[ROWS + 1]
    column, in_sems, out_sems = rest[ROWS + 2 :]
    _, y, _ = place()
    loads = []
    for at, distance in enumerate(PIECES):
        row = (y + distance) & (ROWS - 1)
        loads.append(
            pltpu.make_async_copy(
                pieces[at], column.at[pl.ds(2 * row, 2)], in_sems.at[at]
            )
        )
    far = (y + ROWS // 2) & (ROWS - 1)
    for side in range(2):
        at = ROWS - 1 + side
        rows = column.at[pl.ds(2 * far + side, 1)]
        loads.append(pltpu.make_async_copy(pieces[at], rows, in_sems.at[at]))
    for load in loads:
        load.start()
    for load in loads:
        load.wait()

    def each(act):
        def body(i, _):
            who = served[i]

            @pl.when(who > 0)
            def _():
                pair = 2 * (i & (ROWS - 1)) + who - 1
                act(pltpu.make_async_copy(column.at[pair], out.at[i], out_sems.at[i]))

            return 0

        lax.fori_loop(0, COLS * ROWS, body, 0)

    each(lambda copy: copy.start())
    each(lambda copy: copy.wait())


def combine_kernel(distances, served, arrived, *rest):
    outs, (slots, sems) = rest[: len(distances)], rest[len(distances) :]
    _, y, _ = place()
    order = [distance for group in distances for distance, _ in group]

    def fetches(at, act):
        row = (y + order[at]) & (ROWS - 1)
        for giver_x in range(COLS):
            copy = pltpu.make_async_copy(
                arrived.at[giver_x * ROWS + row],
                slots.at[at * COLS + giver_x],
                sems.at[at * COLS + giver_x],
            )
            pl.when(served[giver_x * ROWS + row] > 0)(functools.partial(act, copy))

    for at in range(len(order)):
        fetches(at, lambda copy: copy.start())
    at = 0
    for out, group in zip(outs, distances):
        put = 0
        for distance, sides in group:
            fetches(at, lambda copy: copy.wait())
            row = (y + distance) & (ROWS - 1)
            for chunk in range(0, R, 64):
                part = pl.ds(chunk, 64)
                totals = [jnp.zeros((64, R), F32) for _ in sides]
                for giver_x in range(COLS):
                    value = slots[at * COLS + giver_x, part, :].astype(F32)
                    who = served[giver_x * ROWS + row]
                    for i, side in enumerate(sides):
                        totals[i] += jnp.where(who == 1 + side, value, 0.0)
                for i, total in enumerate(totals):
                    out[put + i, part, :] = total.astype(BF)
            put += len(sides)
            at += 1


def fold_kernel(got_up, got_down, far_up, far_down, own_up, own_down, send_up, send_down):
    for side in range(2):
        ups = own_up[side].astype(F32) + got_up[side].astype(F32)
        downs = own_down[side].astype(F32) + got_down[side].astype(F32)
        if side == 0:
            ups += far_up[0].astype(F32)
        else:
            downs += far_down[0].astype(F32)
        send_up[side] = ups.astype(BF)
        send_down[side] = downs.astype(BF)


def project(s, a):
    half = jnp.dot(s, a, preferred_element_type=F32).astype(BF)
    return times_transposed(half, s)


def gap_matrix(virt, gap, pair):
    energy = jnp.broadcast_to(virt[pl.ds(pair, 1), :], (R, R))
    return energy + energy.T + gap[pair]


def edge_kernel(
    edge_local, edge_coupling, gap, masked, integrals, virt, edge_inter, lower, upper, partial
):
    pair = pl.program_id(0)
    total = edge_coupling[pair, 0] * project(edge_inter[0, 0], lower[edge_local[pair, 0]])
    total += edge_coupling[pair, 1] * project(edge_inter[0, 1], upper[edge_local[pair, 1]])
    own = masked[0].astype(F32)
    partial[0] = integrals[0].astype(F32) + gap_matrix(virt, gap, pair) * own - total


def gather_kernel(partial, *rest):
    terms, out = rest[:-1], rest[-1]
    total = partial[0]
    for ref in terms:
        total -= ref[0].astype(F32)
    out[0] = total


def final_kernel(
    bucket,
    nbr,
    coupling,
    gap,
    masked,
    partial,
    virt,
    inter,
    named,
    residual,
    new_amps,
    partners,
    sems,
):
    dev, _, _ = place()
    pair = pl.program_id(0)

    def partner_copy(index, entry):
        slot = slot_of(nbr[entry, 2 * dev + index // NBR] >> 1)
        return pltpu.make_async_copy(named.at[slot], partners.at[index], sems.at[index])

    @pl.when(pair == 0)
    def _():
        for index in range(2 * NBR):
            partner_copy(index, index % NBR).start()

    for entry in range(NBR):
        partner_copy(pair * NBR + entry, entry).wait()

    halves = []
    for entry in range(NBR):
        partner = partners[pair * NBR + entry]
        half = jnp.dot(inter[0, entry], partner, preferred_element_type=F32)
        halves.append(half.astype(BF))
    total = partial[0]
    for entry in range(NBR):
        total -= coupling[pair, entry] * times_transposed(halves[entry], inter[0, entry])
    keep = keep_square(jnp.left_shift(32, bucket[2 * dev + pair]))
    value = jnp.where(keep, total, 0.0)
    residual[0] = value
    change = value / gap_matrix(virt, gap, pair)
    new_amps[0] = jnp.where(keep, masked[0].astype(F32) - change, 0.0).astype(BF)


def local(
    amplitudes,
    integrals,
    virt_energy,
    pair_gap,
    rank_bucket,
    neighbours,
    intersection,
    coupling,
    edge_local,
    edge_intersection,
    edge_coupling,
):
    groups = lax.axis_size("grp")
    devices = lax.axis_size("dev")
    nbr = neighbours.T
    rows = [[y * COLS + x for x in range(COLS)] for y in range(ROWS)]

    def swap_columns(value):
        return lax.all_to_all(value, "dev", 0, 0, tiled=True, axis_index_groups=rows)

    def along_y(value, o):
        perm = [(i, (i + o * COLS) % devices) for i in range(devices)]
        return lax.ppermute(value, "dev", perm)

    block = jax.ShapeDtypeStruct((COLS * ROWS, R, R), BF)
    masked, outgoing = pl.pallas_call(
        return_kernel,
        grid=(2,),
        in_specs=[
            SMEM,
            SMEM,
            SMEM,
            pl.BlockSpec((1, R, R), lambda i: (i, 0, 0)),
            pl.BlockSpec((1, NBR, R, R), lambda i: (i, 0, 0, 0)),
        ],
        out_specs=[pl.BlockSpec((1, R, R), lambda i: (i, 0, 0)), ANY],
        out_shape=[jax.ShapeDtypeStruct((2, R, R), BF), block],
        scratch_shapes=[
            pltpu.VMEM((2 * NBR, R, R), BF),
            pltpu.SemaphoreType.DMA((2 * NBR,)),
        ],
        compiler_params=pltpu.CompilerParams(vmem_limit_bytes=LIMIT),
        name="returned_terms",
    )(rank_bucket, nbr, coupling, amplitudes, intersection)
    arrived = swap_columns(outgoing)
    params = pltpu.CompilerParams(vmem_limit_bytes=LIMIT)
    above2, below2 = along_y(masked, -2), along_y(masked, 2)
    above1, below1 = along_y(masked, -1), along_y(masked, 1)
    served = pl.pallas_call(
        served_kernel,
        in_specs=[SMEM],
        out_specs=SMEM,
        out_shape=jax.ShapeDtypeStruct((COLS * ROWS + 1,), jnp.int32),
        name="served_pairs",
    )(nbr)
    above3, below3 = along_y(above2, -1), along_y(below2, 1)
    above4, below4 = along_y(above2[:1], -2), along_y(below2[1:], 2)
    pieces = (masked, above1, below1, above2, below2, above3, below3, above4, below4)
    lower = lax.ppermute(masked, "grp", [(i, i + 1) for i in range(groups - 1)])
    upper = lax.ppermute(masked, "grp", [(i + 1, i) for i in range(groups - 1)])
    served, lower, upper = lax.optimization_barrier((served, lower, upper))
    chosen = pl.pallas_call(
        select_kernel,
        in_specs=[SMEM] + [ANY] * (ROWS + 1),
        out_specs=ANY,
        out_shape=block,
        scratch_shapes=[
            pltpu.VMEM((2 * ROWS, R, R), BF),
            pltpu.SemaphoreType.DMA((ROWS + 1,)),
            pltpu.SemaphoreType.DMA((COLS * ROWS,)),
        ],
        compiler_params=params,
        name="named_pairs",
    )(served, *pieces)
    named = swap_columns(chosen)

    def pairs(count):
        return jax.ShapeDtypeStruct((count, R, R), BF)

    def column_terms(*groups):
        counts = [sum(len(sides) for _, sides in group) for group in groups]
        rows_in = COLS * sum(len(group) for group in groups)
        return pl.pallas_call(
            functools.partial(combine_kernel, groups),
            in_specs=[SMEM, ANY],
            out_specs=[VMEM] * len(groups),
            out_shape=[pairs(count) for count in counts],
            scratch_shapes=[
                pltpu.VMEM((rows_in, R, R), BF),
                pltpu.SemaphoreType.DMA((rows_in,)),
            ],
            compiler_params=pltpu.CompilerParams(vmem_limit_bytes=16 << 20),
            name="column_terms",
        )(served, arrived)

    both = (0, 1)
    up, down, far_up, far_down = column_terms(
        ((1, both), (3, both)), ((-1, both), (-3, both)), ((4, (0,)),), ((4, (1,)),)
    )
    got_up, got_down = along_y(up, 1), along_y(down, -1)
    got_far_up, got_far_down = along_y(far_up, 2), along_y(far_down, -2)
    own, own_up, own_down = column_terms(((0, both),), ((2, both),), ((-2, both),))
    single = pl.BlockSpec((1, R, R), lambda i: (0, 0, 0))
    first = pl.BlockSpec((2, R, R), lambda i: (0, 0, 0))
    second = pl.BlockSpec((2, R, R), lambda i: (1, 0, 0))
    send_up, send_down = pl.pallas_call(
        fold_kernel,
        grid=(1,),
        in_specs=[second, second, single, single, first, first],
        out_specs=[first, first],
        out_shape=[pairs(2)] * 2,
        compiler_params=pltpu.CompilerParams(vmem_limit_bytes=12 << 20),
        name="folded_terms",
    )(got_up, got_down, got_far_up, got_far_down, own_up, own_down)
    terms = [own, got_up, got_down, along_y(send_up, 2), along_y(send_down, -2)]
    each = pl.BlockSpec((1, R, R), lambda i: (i, 0, 0))

    def each_of(count):
        return pl.BlockSpec((1, count, R, R), lambda i: (i, 0, 0, 0))

    partial = pl.pallas_call(
        edge_kernel,
        grid=(2,),
        in_specs=[SMEM] * 3 + [each, each, VMEM, each_of(2), VMEM, VMEM],
        out_specs=each,
        out_shape=jax.ShapeDtypeStruct((2, R, R), F32),
        compiler_params=params,
        name="edges",
    )(
        edge_local,
        edge_coupling,
        pair_gap,
        masked,
        integrals,
        virt_energy,
        edge_intersection,
        lower,
        upper,
    )
    partial = pl.pallas_call(
        gather_kernel,
        grid=(2,),
        in_specs=[each] * (1 + len(terms)),
        out_specs=each,
        out_shape=jax.ShapeDtypeStruct((2, R, R), F32),
        compiler_params=pltpu.CompilerParams(vmem_limit_bytes=12 << 20),
        name="gathered_terms",
    )(partial, *terms)
    outputs = pl.pallas_call(
        final_kernel,
        grid=(2,),
        in_specs=[SMEM] * 4 + [each, each, VMEM, each_of(NBR)] + [ANY],
        out_specs=[each, each],
        out_shape=[
            jax.ShapeDtypeStruct((2, R, R), F32),
            jax.ShapeDtypeStruct((2, R, R), BF),
        ],
        scratch_shapes=[
            pltpu.VMEM((2 * NBR, R, R), BF),
            pltpu.SemaphoreType.DMA((2 * NBR,)),
        ],
        compiler_params=params,
        name="residual_update",
    )(
        rank_bucket,
        nbr,
        coupling,
        pair_gap,
        masked,
        partial,
        virt_energy,
        intersection,
        named,
    )
    return tuple(outputs)


def solution(mesh):
    pair = P(("grp", "dev"))
    placed = (pair, pair, pair, pair, P("grp"), P("grp")) + (pair,) * 5
    return jax.shard_map(
        local, mesh=mesh, in_specs=placed, out_specs=(pair, pair), check_vma=False
    )
```
